1024 devices in a mesh: expert: 8 (over y_hi, core), ffn: 16 (over z), dp: 8 (over x, y_lo).
Axes of the slice: x: 4, y: 8 (y_hi: 4, y_lo: 2; y = y_hi * 2 + y_lo), z: 16, core: 2. Of those that a mesh axis runs over, the one named last changes fastest.
Arguments:
- tokens: bfloat16 [768, 5120], P('expert', 'ffn'), may hold values from -6 to 6
- cotangent: bfloat16 [768, 5120], P('expert', 'ffn'), may hold values from -1.5 to 1.5
- routing: int32 [768, 1], P('expert'), may hold values from 0 to 7; in each aligned block of 96 rows (0 to 95, 96 to 191, ...) at most 24 rows name the same one
- gate_value: float32 [768], P('expert'), may hold values from 0.1 to 0.95
- expert_gate: bfloat16 [8, 5120, 8192], P('expert', 'ffn', 'dp'), may hold values from -0.078125 to 0.078125
- expert_up: bfloat16 [8, 5120, 8192], P('expert', 'ffn', 'dp'), may hold values from -0.078125 to 0.078125
- expert_down: bfloat16 [8, 8192, 5120], P('expert', 'dp', 'ffn'), may hold values from -0.0625 to 0.0625
- shared_gate: bfloat16 [5120, 8192], P('ffn', 'dp'), may hold values from -0.078125 to 0.078125
- shared_up: bfloat16 [5120, 8192], P('ffn', 'dp'), may hold values from -0.078125 to 0.078125
- shared_down: bfloat16 [8192, 5120], P('dp', 'ffn'), may hold values from -0.0625 to 0.0625
Outputs:
- layer_output: bfloat16 [768, 5120], P(('expert', 'dp'), 'ffn')
- grad_tokens: bfloat16 [768, 5120], P(('expert', 'dp'), 'ffn')
- grad_gate: bfloat16 [8, 5120, 8192], P('expert', 'ffn', 'dp')
- grad_up: bfloat16 [8, 5120, 8192], P('expert', 'ffn', 'dp')
The draws below stay inside these ranges and needn't reach their ends.
Inputs may be any that keep to these rules, and one draw needn't show every extreme that they name: `routing`: in each source block of 96 tokens at most 24 tokens share a routed expert, and some block reaches 24.
All inputs are finite; a program needn't handle non-finite values.
Results may differ from the reference program's by a relative error of at most 0.0058.
Values may be sent and summed in bfloat16 or wider, within the bound.
A program may use at most 32 MiB of HBM per device.

```python
import math
import jax
import jax.numpy as jnp
import numpy as np
from jax import lax

D = 5120
FF = 8192
FS = 8192
TOK_DEV = 96
EXPERTS = 8
CAP = 24
SLOTS = 192
TOKENS = 768
N_EXPERT = 8
N_FFN = 16
N_DP = 8


def block_levels(stream_key, extent, split, smallest, top_value):
    level = 1.0
    for dim, parts in split:
        steps = jax.random.uniform(jax.random.fold_in(jax.random.fold_in(stream_key, 6), dim), (parts,), jnp.float32, smallest / len(split), top_value / len(split))
        level = level * jnp.repeat(jnp.exp(steps), extent[dim] // parts).reshape((-1,) + (1,) * (len(extent) - 1 - dim))
    return level


def deal_out(key, own, number, rows, number_of, top, most, slope):
    ranking = jax.random.permutation(key, number_of)
    heavy_load, ordinary = portions_of(number_of, rows * top, most, slope, True), portions_of(number_of, rows * top, most, slope, False)
    places = jnp.arange(number_of)

    def named(lengths, turn):
        used = int((lengths > 0).sum())
        fixed = max(1, used // 4)
        moved = fixed + (places - fixed + turn * (used - fixed)) % max(1, number_of - fixed)
        return jnp.zeros((number_of,), jnp.int32).at[ranking[jnp.where(places < fixed, places, moved)]].set(jnp.asarray(lengths, jnp.int32))

    lengths = jnp.where(number % 4 == 0, named(heavy_load, number // 4), named(ordinary, number - number // 4 - 1))
    mixed = jax.random.permutation(jax.random.fold_in(own, 3), number_of)
    giver, sink = mixed[0:number_of // 2 * 2:2], mixed[1:number_of // 2 * 2:2]
    room = jnp.minimum(lengths[giver] - 1, most - lengths[sink]) // 2
    room = jnp.where((giver == ranking[0]) | (sink == ranking[0]) | (lengths[sink] == 0), 0, jnp.maximum(room, 0))
    moved = jax.random.randint(jax.random.fold_in(own, 4), (number_of // 2,), 0, 1 << 20) % (room + 1)
    lengths = lengths.at[giver].add(-moved).at[sink].add(moved)
    members = jnp.searchsorted(jnp.cumsum(lengths), jnp.arange(rows * top), side="right").astype(jnp.int32)
    table = members.reshape(top, rows).T
    table = table[jax.random.permutation(jax.random.fold_in(own, 1), rows)]
    turn = jax.random.randint(jax.random.fold_in(own, 2), (rows, 1), 0, top)
    return jnp.take_along_axis(table, (jnp.arange(top)[None, :] + turn) % top, axis=1)


def portions_of(number_of, total, reach, lean, full):
    loads = [(1 << 20) // math.isqrt(standing ** lean) + 1 for standing in range(1, number_of + 1)]
    largest = reach if full else min(reach, max(-(-total // number_of), total * loads[0] // sum(loads)))
    least = 1 if total - largest >= number_of - 1 else 0
    counts, rest = [largest] + [least] * (number_of - 1), total - largest - least * (number_of - 1)
    while rest > 0:
        movable = [i for i in range(1, number_of) if counts[i] < largest] or [i for i in range(1, number_of) if counts[i] < reach]
        mass, budget = sum([loads[i] for i in movable]), rest
        for i in movable:
            addition = min(reach - counts[i], max(1, budget * loads[i] // mass), rest)
            counts[i] = counts[i] + addition
            rest = rest - addition
    return np.array(counts)


def centred(rng, shape, scale, most, shards=(), kind=jnp.bfloat16):
    values = scale * jax.random.normal(rng, shape, jnp.float32)
    if shards:
        values = values * block_levels(rng, shape, shards, -0.22, 0.18)
    return jnp.clip(values, -most, most).astype(kind)


def setup_inputs(seed: int = 0) -> dict:
    arg_keys = jax.random.split(jax.random.key(seed), 11)
    tokens = centred(arg_keys[0], (TOKENS, D), 1.0, 6.0, ((0, 8), (1, 16)))
    cotangent = centred(arg_keys[1], (TOKENS, D), 0.25, 1.5, ((0, 8), (1, 16)))
    routing_keys = jax.random.split(jax.random.fold_in(arg_keys[2], 1), TOKENS // TOK_DEV)
    routing_turns = jax.random.permutation(jax.random.fold_in(arg_keys[2], 3), TOKENS // TOK_DEV)
    routing = jax.vmap(lambda own, number: deal_out(jax.random.fold_in(arg_keys[2], 2), own, number, TOK_DEV, EXPERTS, 1, CAP, 2))(routing_keys, routing_turns).reshape((TOKENS, 1))
    gate_value = jnp.clip(0.1 + 0.84999999 * jax.random.uniform(arg_keys[3], (TOKENS,), jnp.float32) ** block_levels(arg_keys[3], (TOKENS,), ((0, 8),), -0.2, 0.2), 0.1, 0.95)
    expert_gate = centred(arg_keys[4], (EXPERTS, D, FF), D ** -0.5, 0.078125, ((0, 8), (1, 16), (2, 8)))
    expert_up = centred(arg_keys[5], (EXPERTS, D, FF), D ** -0.5, 0.078125, ((0, 8), (1, 16), (2, 8)))
    expert_down = centred(arg_keys[6], (EXPERTS, FF, D), FF ** -0.5, 0.0625, ((0, 8), (1, 8), (2, 16)))
    shared_gate = centred(arg_keys[7], (D, FS), D ** -0.5, 0.078125, ((0, 16), (1, 8)))
    shared_up = centred(arg_keys[8], (D, FS), D ** -0.5, 0.078125, ((0, 16), (1, 8)))
    shared_down = centred(arg_keys[9], (FS, D), FS ** -0.5, 0.0625, ((0, 8), (1, 16)))
    return {"tokens": tokens, "cotangent": cotangent, "routing": routing, "gate_value": gate_value, "expert_gate": expert_gate, "expert_up": expert_up, "expert_down": expert_down, "shared_gate": shared_gate, "shared_up": shared_up, "shared_down": shared_down}


def split_sum(factor_pairs, pieces, rounding):
    summed = None
    for operand, weights in factor_pairs:
        row_count = operand.shape[0]
        inner_width = operand.shape[1] // pieces
        left_terms = operand.astype(jnp.float32).reshape(row_count, pieces, inner_width)
        right_terms = weights.astype(jnp.float32).reshape(pieces, inner_width, weights.shape[1])
        products = jnp.einsum("rpk,pkn->prn", left_terms, right_terms)
        summed = products if summed is None else summed + products
    if rounding:
        summed = lax.optimization_barrier(summed.astype(jnp.bfloat16)).astype(jnp.float32)
    return jnp.sum(summed, axis=0)


def swiglu_back(grad_pre, gate_pre, up_pre):
    squash = jax.nn.sigmoid(gate_pre)
    grad_gate_h = (grad_pre * up_pre * squash * (1.0 + gate_pre * (1.0 - squash))).astype(jnp.bfloat16)
    grad_up_h = (grad_pre * (gate_pre * squash)).astype(jnp.bfloat16)
    return grad_gate_h, grad_up_h


def reference(tokens, cotangent, routing, gate_value, expert_gate, expert_up, expert_down, shared_gate, shared_up, shared_down):
    chosen = routing[:, 0]
    blocks = chosen.reshape(N_EXPERT, TOK_DEV)
    onehot = (blocks[:, :, None] == jnp.arange(EXPERTS, dtype=jnp.int32)[None, None, :]).astype(jnp.int32)
    earlier = jnp.cumsum(onehot, axis=1) - onehot
    slot_index = jnp.sum(earlier * onehot, axis=2).reshape(TOKENS).astype(jnp.int32)
    position = (jnp.arange(TOKENS, dtype=jnp.int32) // TOK_DEV) * CAP + slot_index
    slot_table = jnp.full((EXPERTS, SLOTS), TOKENS, dtype=jnp.int32)
    slot_table = slot_table.at[chosen, position].set(jnp.arange(TOKENS, dtype=jnp.int32))
    scaled = (gate_value[:, None] * cotangent.astype(jnp.float32)).astype(jnp.bfloat16)
    zero_row = jnp.zeros((1, D), jnp.bfloat16)
    padded_tokens = jnp.concatenate([tokens, zero_row], axis=0)
    padded_cot = jnp.concatenate([scaled, zero_row], axis=0)

    def one_expert(expert_id):
        source_rows = slot_table[expert_id]
        routed_in = padded_tokens[source_rows]
        routed_cot = padded_cot[source_rows]
        gate_pre = split_sum([(routed_in, expert_gate[expert_id])], N_FFN, False)
        up_pre = split_sum([(routed_in, expert_up[expert_id])], N_FFN, False)
        hidden = (gate_pre * jax.nn.sigmoid(gate_pre) * up_pre).astype(jnp.bfloat16)
        routed_out = split_sum([(hidden, expert_down[expert_id])], N_DP, True)
        grad_pre = split_sum([(routed_cot, expert_down[expert_id].T)], N_FFN, False)
        grad_gate_h, grad_up_h = swiglu_back(grad_pre, gate_pre, up_pre)
        grad_gate = jnp.dot(routed_in.T, grad_gate_h, preferred_element_type=jnp.float32).astype(jnp.bfloat16)
        grad_up = jnp.dot(routed_in.T, grad_up_h, preferred_element_type=jnp.float32).astype(jnp.bfloat16)
        routed_back = split_sum([(grad_gate_h, expert_gate[expert_id].T), (grad_up_h, expert_up[expert_id].T)], N_DP, True)
        return routed_out, routed_back, grad_gate, grad_up

    routed_out, routed_back, grad_gate, grad_up = lax.map(one_expert, jnp.arange(EXPERTS, dtype=jnp.int32))
    routed_tok = routed_out[chosen, position]
    back_tok = routed_back[chosen, position]
    shared_gate_pre = split_sum([(tokens, shared_gate)], N_FFN, False)
    shared_up_pre = split_sum([(tokens, shared_up)], N_FFN, False)
    shared_hidden = (shared_gate_pre * jax.nn.sigmoid(shared_gate_pre) * shared_up_pre).astype(jnp.bfloat16)
    shared_out = jnp.dot(shared_hidden, shared_down, preferred_element_type=jnp.float32)
    shared_grad_pre = split_sum([(cotangent, shared_down.T)], N_FFN, False)
    shared_grad_gate_h, shared_grad_up_h = swiglu_back(shared_grad_pre, shared_gate_pre, shared_up_pre)
    shared_back = jnp.dot(shared_grad_gate_h, shared_gate.T, preferred_element_type=jnp.float32) + jnp.dot(shared_grad_up_h, shared_up.T, preferred_element_type=jnp.float32)
    layer_output = (gate_value[:, None] * routed_tok + shared_out).astype(jnp.bfloat16)
    grad_tokens = (back_tok + shared_back).astype(jnp.bfloat16)
    return layer_output, grad_tokens, grad_gate, grad_up
```

```python
import functools

import jax
import jax.numpy as jnp
from jax import lax
from jax.experimental import pallas as pl
from jax.experimental.pallas import tpu as pltpu
from jax.sharding import PartitionSpec as P

MESH = pl.DeviceIdType.MESH
F32 = jnp.float32
BF16 = jnp.bfloat16

TOK = 96
CAP = 24
NE = 8
NF = 16
ND = 8
SLOTS = NE * CAP
WIDTH = 320
HID = 1024
SUB = 48
COL = 128
STREAMS = 3
HOPS = (8, 7)
NARROW = (6, 4)
WIDE = max(HOPS[0] - NARROW[0], HOPS[1] - NARROW[1])
ROWS_DP = TOK // ND


def dot(a, b):
    return lax.dot_general(a, b, (((1,), (0,)), ((), ())), preferred_element_type=F32)


def dot_last(a, b):
    return lax.dot_general(a, b, (((1,), (1,)), ((), ())), preferred_element_type=F32)


def dot_first(a, b):
    return lax.dot_general(a, b, (((0,), (0,)), ((), ())), preferred_element_type=F32)


def kernel(
    tok_hbm, cot_hbm, routing_hbm, gate_hbm, eg_hbm, eu_hbm, ed_hbm, sg_hbm, su_hbm, sd_hbm,
    lo_hbm, gt_hbm, gg_hbm, gu_hbm,
    tok, cot, routing, gate, eg, eu, ed, sg, su, sd,
    outbox, inbox, routed_in, routed_cot, part_s, part_r,
    stage_b, stage_f, held_b, held_f, act_s, act_r,
    outbox2, inbox2, term, outbox3, inbox3, lo, gt, gg, gu,
    load_sem, store_sem, rs_send, rs_recv, ag_send, ag_recv, x_send, x_recv, y_send, y_recv, z_send, z_recv,
):
    me_e, me_f, me_d = lax.axis_index("expert"), lax.axis_index("ffn"), lax.axis_index("dp")
    nbr = (lax.rem(me_f + 1, NF), lax.rem(me_f + NF - 1, NF))

    loads = [
        pltpu.make_async_copy(src, dst, load_sem.at[n])
        for n, (src, dst) in enumerate(
            [
                (routing_hbm, routing), (gate_hbm, gate), (tok_hbm, tok), (cot_hbm, cot),
                (sg_hbm, sg), (su_hbm, su), (sd_hbm, sd),
                (eg_hbm.at[0], eg), (eu_hbm.at[0], eu), (ed_hbm.at[0], ed),
            ]
        )
    ]
    for load in loads:
        load.start()

    barrier = pltpu.get_barrier_semaphore()
    for other in nbr:
        pl.semaphore_signal(barrier, inc=1, device_id={"ffn": other}, device_id_type=MESH)
    for k in range(1, NE):
        pl.semaphore_signal(
            barrier, inc=1, device_id={"expert": lax.rem(me_e + k, NE)}, device_id_type=MESH
        )
    for k in range(1, ND):
        pl.semaphore_signal(
            barrier, inc=1, device_id={"dp": lax.rem(me_d + k, ND)}, device_id_type=MESH
        )

    for n in range(4):
        loads[n].wait()
    chosen = routing[...]
    onehot = (chosen == lax.broadcasted_iota(jnp.int32, (TOK, NE), 1)).astype(F32)
    before = (
        lax.broadcasted_iota(jnp.int32, (TOK, TOK), 0) > lax.broadcasted_iota(jnp.int32, (TOK, TOK), 1)
    )
    earlier = dot(before.astype(BF16), onehot.astype(BF16))
    slot = jnp.sum(earlier * onehot, axis=1, keepdims=True).astype(jnp.int32)
    target = chosen * (2 * CAP) + slot
    boxes = lax.broadcasted_iota(jnp.int32, (TOK, 2 * SLOTS), 1)
    pick_first = (boxes == target).astype(BF16)
    pick_second = (boxes == target + CAP).astype(BF16)
    same = (
        lax.broadcasted_iota(jnp.int32, (TOK, TOK), 0) == lax.broadcasted_iota(jnp.int32, (TOK, TOK), 1)
    )
    gate_column = jnp.sum(
        jnp.where(same, jnp.broadcast_to(gate[...].reshape(1, TOK), (TOK, TOK)), 0.0), axis=1, keepdims=True
    )
    scaled = (gate_column * cot[...].astype(F32)).astype(BF16)
    outbox[...] = (dot_first(pick_first, tok[...]) + dot_first(pick_second, scaled)).astype(BF16)

    pl.semaphore_wait(barrier, 2 + (NE - 1) + (ND - 1))

    def box(ref, index):
        return ref.at[pl.ds(pl.multiple_of(index * 2 * CAP, 2 * CAP), 2 * CAP)]

    def exchange(source, target_ref, send, recv, k):
        peer = lax.rem(me_e + k, NE)
        return pltpu.make_async_remote_copy(
            src_ref=box(source, peer), dst_ref=box(target_ref, me_e),
            send_sem=send.at[k], recv_sem=recv.at[k],
            device_id={"expert": peer}, device_id_type=MESH,
        )

    def arrival(source, target_ref, send, recv, k):
        peer = lax.rem(me_e + NE - k, NE)
        return pltpu.make_async_remote_copy(
            src_ref=box(source, me_e), dst_ref=box(target_ref, peer),
            send_sem=send.at[k], recv_sem=recv.at[k],
            device_id={"expert": peer}, device_id_type=MESH,
        )

    for k in range(1, NE):
        exchange(outbox, inbox, x_send, x_recv, k).start()
    box(inbox, me_e)[...] = box(outbox, me_e)[...]

    for n in range(4, 7):
        loads[n].wait()
    part_s[0] = dot(tok[...], sg[...])
    part_s[1] = dot(tok[...], su[...])
    part_s[2] = dot_last(cot[...], sd[...])

    def block(ref, stream, owner):
        columns = pl.ds(pl.multiple_of(lax.div(owner, 2) * COL, COL), COL)
        half = lax.rem(owner, 2)
        if stream == 0:
            first = half * SUB
        else:
            first = half * 2 * SUB + (stream - 1) * SUB
        return ref.at[:, pl.ds(pl.multiple_of(first, SUB), SUB), columns]

    def mine(stream):
        return (part_s if stream == 0 else part_r), (act_s if stream == 0 else act_r)

    def slots(narrow, wide, stream, way, step):
        if step < NARROW[way]:
            return narrow.at[stream, way, step]
        return wide.at[stream, way, step - NARROW[way]]

    def sum_copy(stream, way, step):
        return pltpu.make_async_remote_copy(
            src_ref=slots(stage_b, stage_f, stream, way, step),
            dst_ref=slots(held_b, held_f, stream, way, step),
            send_sem=rs_send.at[stream, way, step], recv_sem=rs_recv.at[stream, way, step],
            device_id={"ffn": nbr[way]}, device_id_type=MESH,
        )

    def sum_step(stream, way, step):
        if way == 0:
            owner = lax.rem(me_f + HOPS[0] - step, NF)
        else:
            owner = lax.rem(me_f + NF - HOPS[1] + step, NF)
        value = block(mine(stream)[0], stream, owner)[...]
        if step > 0:
            sum_copy(stream, way, step - 1).wait_recv()
            value = value + slots(held_b, held_f, stream, way, step - 1)[...].astype(F32)
        stage = slots(stage_b, stage_f, stream, way, step)
        stage[...] = value.astype(stage.dtype)
        sum_copy(stream, way, step).start()

    def sum_end(stream):
        part, act = mine(stream)
        value = block(part, stream, me_f)[...]
        for way in range(2):
            last = HOPS[way] - 1
            sum_copy(stream, way, last).wait_recv()
            value = value + slots(held_b, held_f, stream, way, last)[...].astype(F32)
        g, u, p = value[0], value[1], value[2]
        squash = jax.nn.sigmoid(g)
        silu = g * squash
        own = block(act, stream, me_f)
        own[0] = (silu * u).astype(BF16)
        own[1] = (p * u * squash * (1.0 + g * (1.0 - squash))).astype(BF16)
        own[2] = (p * silu).astype(BF16)

    def gather_copy(stream, way, step, owner):
        ref = block(mine(stream)[1], stream, owner)
        return pltpu.make_async_remote_copy(
            src_ref=ref, dst_ref=ref,
            send_sem=ag_send.at[stream, way, step], recv_sem=ag_recv.at[stream, way, step],
            device_id={"ffn": nbr[way]}, device_id_type=MESH,
        )

    def gather_owner(way, step):
        return lax.rem(me_f + NF - step, NF) if way == 0 else lax.rem(me_f + step, NF)

    def gather_arrived(stream, way, step):
        gather_copy(stream, way, step, gather_owner(way, step + 1)).wait_recv()

    def gather_step(stream, way, step):
        if step > 0:
            gather_arrived(stream, way, step - 1)
        gather_copy(stream, way, step, gather_owner(way, step)).start()

    def gather_end(stream):
        for way in range(2):
            gather_arrived(stream, way, HOPS[way] - 1)

    def turn(stream, now):
        if now < 0:
            return
        if now < HOPS[0]:
            for way in range(2):
                if now < HOPS[way]:
                    sum_step(stream, way, now)
        elif now < 2 * HOPS[0]:
            if now == HOPS[0]:
                sum_end(stream)
            for way in range(2):
                if now - HOPS[0] < HOPS[way]:
                    gather_step(stream, way, now - HOPS[0])
        elif now == 2 * HOPS[0]:
            gather_end(stream)

    LEAD = 2
    for now in range(LEAD):
        turn(0, now)

    for k in range(1, NE):
        arrival(outbox, inbox, x_send, x_recv, k).wait_recv()
    came = inbox[...].astype(F32)
    routed_in[...] = jnp.concatenate(
        [came[2 * CAP * e : 2 * CAP * e + CAP] for e in range(NE)], axis=0
    ).astype(BF16)
    routed_cot[...] = jnp.concatenate(
        [came[2 * CAP * e + CAP : 2 * CAP * (e + 1)] for e in range(NE)], axis=0
    ).astype(BF16)
    for n in range(7, 10):
        loads[n].wait()
    part_r[0] = dot(routed_in[...], eg[...])
    part_r[1] = dot(routed_in[...], eu[...])
    part_r[2] = dot_last(routed_cot[...], ed[...])

    LAG = 4
    for now in range(LEAD, 2 * HOPS[0] + LEAD + LAG + 1):
        for stream in range(1, STREAMS):
            turn(stream, now - LEAD)
        if now < HOPS[0]:
            turn(0, now)
        else:
            late = now - (LEAD + LAG)
            if late >= HOPS[0]:
                turn(0, late)
        if now - LEAD == 2 * HOPS[0]:
            routed_out = dot(act_r[0], ed[...])
            routed_back = dot_last(act_r[1], eg[...]) + dot_last(act_r[2], eu[...])
            for e in range(NE):
                outbox2[2 * CAP * e : 2 * CAP * (e + 1)] = jnp.concatenate(
                    [routed_out[CAP * e : CAP * (e + 1)], routed_back[CAP * e : CAP * (e + 1)]], axis=0
                ).astype(BF16)
            for k in range(1, NE):
                exchange(outbox2, inbox2, y_send, y_recv, k).start()
            box(inbox2, me_e)[...] = box(outbox2, me_e)[...]

    shared_out = dot(act_s[0], sd[...])
    shared_back = dot_last(act_s[1], sg[...]) + dot_last(act_s[2], su[...])
    for k in range(1, NE):
        arrival(outbox2, inbox2, y_send, y_recv, k).wait_recv()
    term[0] = gate_column * dot(pick_first, inbox2[...]) + shared_out
    term[1] = dot(pick_second, inbox2[...]) + shared_back
    for d in range(ND):
        outbox3[d, :ROWS_DP] = term[0, ROWS_DP * d : ROWS_DP * (d + 1)]
        outbox3[d, ROWS_DP:] = term[1, ROWS_DP * d : ROWS_DP * (d + 1)]

    def dp_send(k):
        peer = lax.rem(me_d + k, ND)
        return pltpu.make_async_remote_copy(
            src_ref=outbox3.at[peer], dst_ref=inbox3.at[k],
            send_sem=z_send.at[k], recv_sem=z_recv.at[k],
            device_id={"dp": peer}, device_id_type=MESH,
        )

    for k in range(1, ND):
        dp_send(k).start()

    gg[...] = dot_first(routed_in[...], act_r[1]).astype(BF16)
    gu[...] = dot_first(routed_in[...], act_r[2]).astype(BF16)
    stores = [
        pltpu.make_async_copy(gg, gg_hbm.at[0], store_sem.at[0]),
        pltpu.make_async_copy(gu, gu_hbm.at[0], store_sem.at[1]),
    ]
    for store in stores:
        store.start()

    total = outbox3[me_d]
    for k in range(1, ND):
        dp_send(k).wait_recv()
        total = total + inbox3[k]
    lo[...] = total[:ROWS_DP].astype(BF16)
    gt[...] = total[ROWS_DP:].astype(BF16)
    last = [
        pltpu.make_async_copy(lo, lo_hbm, store_sem.at[2]),
        pltpu.make_async_copy(gt, gt_hbm, store_sem.at[3]),
    ]
    for store in last:
        store.start()
    for stream in range(STREAMS):
        for way in range(2):
            for step in range(HOPS[way]):
                sum_copy(stream, way, step).wait_send()
                gather_copy(stream, way, step, gather_owner(way, step)).wait_send()
    for k in range(1, NE):
        exchange(outbox, inbox, x_send, x_recv, k).wait_send()
        exchange(outbox2, inbox2, y_send, y_recv, k).wait_send()
    for k in range(1, ND):
        dp_send(k).wait_send()
    for store in stores + last:
        store.wait()


def per_device(*args):
    vmem = pltpu.VMEM
    dma = pltpu.SemaphoreType.DMA
    any_spec = pl.BlockSpec(memory_space=pl.ANY)
    return pl.pallas_call(
        kernel,
        out_shape=(
            jax.ShapeDtypeStruct((ROWS_DP, WIDTH), BF16),
            jax.ShapeDtypeStruct((ROWS_DP, WIDTH), BF16),
            jax.ShapeDtypeStruct((1, WIDTH, HID), BF16),
            jax.ShapeDtypeStruct((1, WIDTH, HID), BF16),
        ),
        in_specs=[any_spec] * 10,
        out_specs=(any_spec,) * 4,
        scratch_shapes=[
            vmem((TOK, WIDTH), BF16), vmem((TOK, WIDTH), BF16), vmem((TOK, 1), jnp.int32), vmem((TOK,), F32),
            vmem((WIDTH, HID), BF16), vmem((WIDTH, HID), BF16), vmem((HID, WIDTH), BF16),
            vmem((WIDTH, HID), BF16), vmem((WIDTH, HID), BF16), vmem((HID, WIDTH), BF16),
            vmem((2 * SLOTS, WIDTH), BF16), vmem((2 * SLOTS, WIDTH), BF16),
            vmem((SLOTS, WIDTH), BF16), vmem((SLOTS, WIDTH), BF16),
            vmem((3, TOK, HID), F32), vmem((3, SLOTS, HID), F32),
            vmem((STREAMS, 2, max(NARROW), 3, SUB, COL), BF16), vmem((STREAMS, 2, WIDE, 3, SUB, COL), F32),
            vmem((STREAMS, 2, max(NARROW), 3, SUB, COL), BF16), vmem((STREAMS, 2, WIDE, 3, SUB, COL), F32),
            vmem((3, TOK, HID), BF16), vmem((3, SLOTS, HID), BF16),
            vmem((2 * SLOTS, WIDTH), BF16), vmem((2 * SLOTS, WIDTH), BF16),
            vmem((2, TOK, WIDTH), F32),
            vmem((ND, 2 * ROWS_DP, WIDTH), F32), vmem((ND, 2 * ROWS_DP, WIDTH), F32),
            vmem((ROWS_DP, WIDTH), BF16), vmem((ROWS_DP, WIDTH), BF16),
            vmem((WIDTH, HID), BF16), vmem((WIDTH, HID), BF16),
            dma((10,)), dma((4,)),
            dma((STREAMS, 2, HOPS[0])), dma((STREAMS, 2, HOPS[0])),
            dma((STREAMS, 2, HOPS[0])), dma((STREAMS, 2, HOPS[0])),
            dma((NE,)), dma((NE,)), dma((NE,)), dma((NE,)), dma((ND,)), dma((ND,)),
        ],
        compiler_params=pltpu.CompilerParams(
            collective_id=0, has_side_effects=True, vmem_limit_bytes=48 * 1024 * 1024
        ),
    )(*args)


def solution(mesh):
    placed = (
        P("expert", "ffn"),
        P("expert", "ffn"),
        P("expert", None),
        P("expert"),
        P("expert", "ffn", "dp"),
        P("expert", "ffn", "dp"),
        P("expert", "dp", "ffn"),
        P("ffn", "dp"),
        P("ffn", "dp"),
        P("dp", "ffn"),
    )
    return jax.shard_map(
        per_device,
        mesh=mesh,
        in_specs=placed,
        out_specs=(
            P(("expert", "dp"), "ffn"),
            P(("expert", "dp"), "ffn"),
            P("expert", "ffn", "dp"),
            P("expert", "ffn", "dp"),
        ),
        check_vma=False,
    )
```

```python
import functools

import jax
import jax.numpy as jnp
from jax import lax
from jax.experimental import pallas as pl
from jax.experimental.pallas import tpu as pltpu
from jax.sharding import PartitionSpec as P

MESH = pl.DeviceIdType.MESH
F32 = jnp.float32
BF16 = jnp.bfloat16

TOK = 96
CAP = 24
NE = 8
NF = 16
ND = 8
SLOTS = NE * CAP
WIDTH = 320
HID = 1024
SUB = 48
COL = 128
STREAMS = 3
SUMS = ((0, 8, 4), (1, 7, 3), (0, 3, 1), (1, 2, 1))
SUM_AT = (0.0, 0.01, 2.5, 3.5)
SUM_TIME = 6.5
GATHERS = ((0, 1, 8), (1, 1, 7))
GATHER_AT = (0.0, 0.01)
GATHER_TIME = 8
LINKS = 8
JUMPS = sorted({1} | {near for _, _, near in SUMS} | {near for _, near, _ in GATHERS})
LEAD = 3
STAGGER = 0
SOURCES = ((0, 2, 4, 6), (1, 3, 5, 7))
LATE = 2
ROWS_DP = TOK // ND


def dot(a, b):
    return lax.dot_general(a, b, (((1,), (0,)), ((), ())), preferred_element_type=F32)


def dot_last(a, b):
    return lax.dot_general(a, b, (((1,), (1,)), ((), ())), preferred_element_type=F32)


def dot_first(a, b):
    return lax.dot_general(a, b, (((0,), (0,)), ((), ())), preferred_element_type=F32)


def kernel(
    tok_hbm, cot_hbm, routing_hbm, gate_hbm, eg_hbm, eu_hbm, ed_hbm, sg_hbm, su_hbm, sd_hbm,
    lo_hbm, gt_hbm, gg_hbm, gu_hbm,
    tok, cot, routing, gate, eg, eu, ed, sg, su, sd,
    outbox, inbox, routed_in, routed_cot, part_s, part_r,
    stage, held, act_s, act_r,
    outbox2, inbox2, term, outbox3, inbox3, lo, gt, gg, gu,
    load_sem, store_sem, rs_send, rs_recv, ag_send, ag_recv, x_send, x_recv, y_send, y_recv, z_send, z_recv,
):
    me_e, me_f, me_d = lax.axis_index("expert"), lax.axis_index("ffn"), lax.axis_index("dp")
    y_hi, core = lax.div(me_e, 2), lax.rem(me_e, 2)
    y_lo = lax.rem(me_d, 2)
    other_d = me_d + 1 - 2 * y_lo
    toward = 2 * y_lo - 1

    def way_of(way, stream):
        return 1 - way if stream == STREAMS - 1 else way

    def along(way, distance):
        return lax.rem(me_f + (distance if way == 0 else NF - distance), NF)

    def expert_at(dy, swap):
        return 2 * lax.rem(y_hi + dy + 4, 4) + (core if swap == 0 else 1 - core)

    loads = [
        pltpu.make_async_copy(src, dst, load_sem.at[n])
        for n, (src, dst) in enumerate(
            [
                (routing_hbm, routing), (gate_hbm, gate), (tok_hbm, tok), (cot_hbm, cot),
                (sg_hbm, sg), (su_hbm, su), (sd_hbm, sd),
                (eg_hbm.at[0], eg), (eu_hbm.at[0], eu), (ed_hbm.at[0], ed),
            ]
        )
    ]
    for load in loads:
        load.start()

    barrier = pltpu.get_barrier_semaphore()
    for jump in JUMPS:
        for way in range(2):
            pl.semaphore_signal(
                barrier, inc=1, device_id={"ffn": along(way, jump)}, device_id_type=MESH
            )
    for dy in (toward, 2):
        for swap in range(2):
            pl.semaphore_signal(
                barrier, inc=1, device_id={"expert": expert_at(dy, swap), "dp": other_d}, device_id_type=MESH
            )
    for k in range(1, NE):
        pl.semaphore_signal(
            barrier, inc=1, device_id={"expert": lax.rem(me_e + k, NE)}, device_id_type=MESH
        )
    for k in range(1, ND):
        pl.semaphore_signal(
            barrier, inc=1, device_id={"dp": lax.rem(me_d + k, ND)}, device_id_type=MESH
        )

    for n in range(4):
        loads[n].wait()

    same = (
        lax.broadcasted_iota(jnp.int32, (TOK, TOK), 0) == lax.broadcasted_iota(jnp.int32, (TOK, TOK), 1)
    )

    def column(row):
        across = jnp.broadcast_to(row.astype(F32).reshape(1, TOK), (TOK, TOK))
        return jnp.sum(jnp.where(same, across, 0.0), axis=1, keepdims=True)

    gate_column = column(gate[...])
    chosen = column(routing[...]).astype(jnp.int32)
    onehot = (chosen == lax.broadcasted_iota(jnp.int32, (TOK, NE), 1)).astype(F32)
    before = (
        lax.broadcasted_iota(jnp.int32, (TOK, TOK), 0) > lax.broadcasted_iota(jnp.int32, (TOK, TOK), 1)
    )
    earlier = dot(before.astype(BF16), onehot.astype(BF16))
    slot = jnp.sum(earlier * onehot, axis=1, keepdims=True).astype(jnp.int32)
    target = chosen * (2 * CAP) + slot
    boxes = lax.broadcasted_iota(jnp.int32, (TOK, 2 * SLOTS), 1)
    pick_first = (boxes == target).astype(BF16)
    pick_second = (boxes == target + CAP).astype(BF16)
    scaled = (gate_column * cot[...].astype(F32)).astype(BF16)
    outbox[...] = (dot_first(pick_first, tok[...]) + dot_first(pick_second, scaled)).astype(BF16)

    for n in range(4, 7):
        loads[n].wait()
    part_s[0] = dot(tok[...], sg[...])
    part_s[1] = dot(tok[...], su[...])
    part_s[2] = dot(cot[...], sd[...])

    pl.semaphore_wait(barrier, 2 * len(JUMPS) + 4 + (NE - 1) + (ND - 1))

    def box(ref, index):
        return ref.at[pl.ds(pl.multiple_of(index * 2 * CAP, 2 * CAP), 2 * CAP)]

    routes = [(0, 0, 1)] + [
        (dy, flip, swap) for dy, flip in ((toward, 1), (toward, 0), (2, 1)) for swap in range(2)
    ]

    def tokens_out(n):
        dy, flip, swap = routes[n]
        peer = expert_at(dy, swap)
        return pltpu.make_async_remote_copy(
            src_ref=box(outbox, peer), dst_ref=box(inbox, me_e),
            send_sem=x_send.at[n], recv_sem=x_recv.at[n],
            device_id={"expert": peer, "dp": other_d if flip else me_d}, device_id_type=MESH,
        )

    def tokens_in(n):
        dy, flip, swap = routes[n]
        peer = expert_at(dy if flip else -dy, swap)
        return pltpu.make_async_remote_copy(
            src_ref=box(outbox, me_e), dst_ref=box(inbox, peer),
            send_sem=x_send.at[n], recv_sem=x_recv.at[n],
            device_id={"expert": peer, "dp": other_d if flip else me_d}, device_id_type=MESH,
        )

    for n in range(len(routes)):
        tokens_out(n).start()
    box(inbox, me_e)[...] = box(outbox, me_e)[...]

    def block(ref, stream, owner):
        columns = pl.ds(pl.multiple_of(lax.div(owner, 2) * COL, COL), COL)
        half = lax.rem(owner, 2)
        first = half * SUB + (0 if stream == 0 else (stream - 1) * 2 * SUB)
        return ref.at[:, pl.ds(pl.multiple_of(first, SUB), SUB), columns]

    def mine(stream):
        return (part_s if stream == 0 else part_r), (act_s if stream == 0 else act_r)

    def sum_copy(stream, chain, step):
        way, far, near = SUMS[chain]
        way = way_of(way, stream)
        return pltpu.make_async_remote_copy(
            src_ref=stage.at[stream, chain, step], dst_ref=held.at[stream, chain, step],
            send_sem=rs_send.at[stream, chain, step], recv_sem=rs_recv.at[stream, chain, step],
            device_id={"ffn": along(way, 1 if step < far - near else near)}, device_id_type=MESH,
        )

    def sum_step(stream, chain, step):
        way, far, _ = SUMS[chain]
        way = way_of(way, stream)
        value = block(mine(stream)[0], stream, along(way, far - step))[...]
        if step > 0:
            sum_copy(stream, chain, step - 1).wait_recv()
            value = value + held[stream, chain, step - 1].astype(F32)
        stage[stream, chain, step] = value.astype(BF16)
        sum_copy(stream, chain, step).start()

    def sum_end(stream):
        part, act = mine(stream)
        value = block(part, stream, me_f)[...]
        for chain, (_, far, near) in sorted(enumerate(SUMS), reverse=True):
            sum_copy(stream, chain, far - near).wait_recv()
            value = value + held[stream, chain, far - near].astype(F32)
        g, u, p = value[0], value[1], value[2]
        squash = jax.nn.sigmoid(g)
        silu = g * squash
        own = block(act, stream, me_f)
        own[0] = (silu * u).astype(BF16)
        own[1] = (p * u * squash * (1.0 + g * (1.0 - squash))).astype(BF16)
        own[2] = (p * silu).astype(BF16)

    def gather_copy(stream, chain, step, distance):
        way, near, _ = GATHERS[chain]
        way = way_of(way, stream)
        ref = block(mine(stream)[1], stream, along(1 - way, distance))
        return pltpu.make_async_remote_copy(
            src_ref=ref, dst_ref=ref,
            send_sem=ag_send.at[stream, chain, step], recv_sem=ag_recv.at[stream, chain, step],
            device_id={"ffn": along(way, near if step == 0 else 1)}, device_id_type=MESH,
        )

    def gather_out(stream, chain, step):
        return gather_copy(stream, chain, step, 0 if step == 0 else GATHERS[chain][1] + step - 1)

    def gather_arrived(stream, chain, step):
        gather_copy(stream, chain, step, GATHERS[chain][1] + step).wait_recv()

    def gather_step(stream, chain, step):
        if step > 0:
            gather_arrived(stream, chain, step - 1)
        gather_out(stream, chain, step).start()

    def gather_end(stream):
        for chain, (_, near, far) in sorted(enumerate(GATHERS), reverse=True):
            gather_arrived(stream, chain, far - near)

    def routed_terms():
        for n in range(len(routes)):
            tokens_in(n).wait_recv()
        came = inbox[...].astype(F32)
        routed_in[...] = jnp.concatenate(
            [came[2 * CAP * e : 2 * CAP * e + CAP] for e in SOURCES[0] + SOURCES[1]], axis=0
        ).astype(BF16)
        routed_cot[...] = jnp.concatenate(
            [came[2 * CAP * e + CAP : 2 * CAP * (e + 1)] for e in SOURCES[0] + SOURCES[1]], axis=0
        ).astype(BF16)
        for n in range(7, 10):
            loads[n].wait()
        part_r[0] = dot(routed_in[...], eg[...])
        part_r[1] = dot(routed_in[...], eu[...])
        part_r[2] = dot(routed_cot[...], ed[...])

    def result_copy(peer, sender):
        return pltpu.make_async_remote_copy(
            src_ref=box(outbox2, peer), dst_ref=box(inbox2, sender),
            send_sem=y_send.at[peer], recv_sem=y_recv.at[sender],
            device_id={"expert": peer}, device_id_type=MESH,
        )

    def routed_results(part):
        rows = slice(part * 2 * SUB, (part + 1) * 2 * SUB)
        routed_out = dot_last(act_r[0, rows], ed[...])
        routed_back = dot_last(act_r[1, rows], eg[...]) + dot_last(act_r[2, rows], eu[...])
        for n, e in enumerate(SOURCES[part]):
            outbox2[2 * CAP * e : 2 * CAP * (e + 1)] = jnp.concatenate(
                [routed_out[CAP * n : CAP * (n + 1)], routed_back[CAP * n : CAP * (n + 1)]], axis=0
            ).astype(BF16)

            @pl.when(me_e != e)
            def _():
                result_copy(e, me_e).start()

            @pl.when(me_e == e)
            def _():
                box(inbox2, e)[...] = box(outbox2, e)[...]

    begins = (0, LEAD + 0.1, LEAD + STAGGER + 0.2)
    routed_end = begins[2] + SUM_TIME + GATHER_TIME
    plan = [(LEAD - 0.5, "Rterms", routed_terms)]
    for stream, begin in enumerate(begins):
        second = begin + SUM_TIME if stream > 0 else routed_end - GATHER_TIME + LATE
        if stream > 0:
            plan.append((second + GATHER_TIME + 0.05, f"Rout{stream}", functools.partial(routed_results, stream - 1)))
        plan.append((begin + SUM_TIME - 0.05, f"Aend{stream}", functools.partial(sum_end, stream)))
        plan.append((second + GATHER_TIME, f"Gend{stream}", functools.partial(gather_end, stream)))
        for chain, (_, far, near) in enumerate(SUMS):
            for step in range(far - near + 1):
                when = begin + SUM_AT[chain] + step
                plan.append((when, f"A{stream}{chain}{step}", functools.partial(sum_step, stream, chain, step)))
        for chain, (_, near, far) in enumerate(GATHERS):
            for step in range(far - near + 1):
                when = second + GATHER_AT[chain] + step
                plan.append((when, f"G{stream}{chain}{step}", functools.partial(gather_step, stream, chain, step)))
    for _, name, act in sorted(plan, key=lambda entry: entry[0]):
        act()

    shared_out = dot_last(act_s[0], sd[...])
    shared_back = dot_last(act_s[1], sg[...]) + dot_last(act_s[2], su[...])
    for k in range(1, NE):
        result_copy(me_e, lax.rem(me_e + k, NE)).wait_recv()
    term[0] = gate_column * dot(pick_first, inbox2[...]) + shared_out
    term[1] = dot(pick_second, inbox2[...]) + shared_back
    for d in range(ND):
        outbox3[d, :ROWS_DP] = term[0, ROWS_DP * d : ROWS_DP * (d + 1)]
        outbox3[d, ROWS_DP:] = term[1, ROWS_DP * d : ROWS_DP * (d + 1)]

    def dp_send(k):
        peer = lax.rem(me_d + k, ND)
        return pltpu.make_async_remote_copy(
            src_ref=outbox3.at[peer], dst_ref=inbox3.at[k],
            send_sem=z_send.at[k], recv_sem=z_recv.at[k],
            device_id={"dp": peer}, device_id_type=MESH,
        )

    for k in range(1, ND):
        dp_send(k).start()

    gg[...] = dot_first(routed_in[...], act_r[1]).astype(BF16)
    gu[...] = dot_first(routed_in[...], act_r[2]).astype(BF16)
    stores = [
        pltpu.make_async_copy(gg, gg_hbm.at[0], store_sem.at[0]),
        pltpu.make_async_copy(gu, gu_hbm.at[0], store_sem.at[1]),
    ]
    for store in stores:
        store.start()

    total = outbox3[me_d]
    for k in range(1, ND):
        dp_send(k).wait_recv()
        total = total + inbox3[k]
    lo[...] = total[:ROWS_DP].astype(BF16)
    gt[...] = total[ROWS_DP:].astype(BF16)
    last = [
        pltpu.make_async_copy(lo, lo_hbm, store_sem.at[2]),
        pltpu.make_async_copy(gt, gt_hbm, store_sem.at[3]),
    ]
    for store in last:
        store.start()
    for stream in range(STREAMS):
        for chain, (_, far, near) in enumerate(SUMS):
            for step in range(far - near + 1):
                sum_copy(stream, chain, step).wait_send()
        for chain, (_, near, far) in enumerate(GATHERS):
            for step in range(far - near + 1):
                gather_out(stream, chain, step).wait_send()
    for n in range(len(routes)):
        tokens_out(n).wait_send()
    for k in range(1, NE):
        result_copy(lax.rem(me_e + k, NE), me_e).wait_send()
    for k in range(1, ND):
        dp_send(k).wait_send()
    for store in stores + last:
        store.wait()


def place(*refs):
    n = (len(refs) - 1) // 3
    sources, results, held, sem = refs[:n], refs[n : 2 * n], refs[2 * n : 3 * n], refs[-1]
    reads = [pltpu.make_async_copy(sources[k], held[k], sem.at[0, k]) for k in range(n)]
    writes = [pltpu.make_async_copy(held[k], results[k], sem.at[1, k]) for k in range(n)]
    for read in reads:
        read.start()
    for read, write in zip(reads, writes):
        read.wait()
        write.start()
    for write in writes:
        write.wait()


def per_device(tokens, cotangent, routing, gate_value, eg, eu, ed, sg, su, sd):
    args = (
        tokens, cotangent, routing.reshape(TOK), gate_value,
        eg, eu, jnp.swapaxes(ed, 1, 2), sg, su, jnp.swapaxes(sd, 0, 1),
    )
    vmem = pltpu.VMEM
    dma = pltpu.SemaphoreType.DMA
    any_spec = pl.BlockSpec(memory_space=pl.ANY)
    hbm_spec = pl.BlockSpec(memory_space=pltpu.HBM)
    results = pl.pallas_call(
        kernel,
        out_shape=(
            jax.ShapeDtypeStruct((ROWS_DP, WIDTH), BF16),
            jax.ShapeDtypeStruct((ROWS_DP, WIDTH), BF16),
            jax.ShapeDtypeStruct((1, WIDTH, HID), BF16),
            jax.ShapeDtypeStruct((1, WIDTH, HID), BF16),
        ),
        in_specs=[hbm_spec] * 10,
        out_specs=(any_spec,) * 4,
        scratch_shapes=[
            vmem((TOK, WIDTH), BF16), vmem((TOK, WIDTH), BF16), vmem((TOK,), jnp.int32), vmem((TOK,), F32),
            vmem((WIDTH, HID), BF16), vmem((WIDTH, HID), BF16), vmem((WIDTH, HID), BF16),
            vmem((WIDTH, HID), BF16), vmem((WIDTH, HID), BF16), vmem((WIDTH, HID), BF16),
            vmem((2 * SLOTS, WIDTH), BF16), vmem((2 * SLOTS, WIDTH), BF16),
            vmem((SLOTS, WIDTH), BF16), vmem((SLOTS, WIDTH), BF16),
            vmem((3, TOK, HID), F32), vmem((3, SLOTS, HID), F32),
            vmem((STREAMS, len(SUMS), LINKS, 3, SUB, COL), BF16),
            vmem((STREAMS, len(SUMS), LINKS, 3, SUB, COL), BF16),
            vmem((3, TOK, HID), BF16), vmem((3, SLOTS, HID), BF16),
            vmem((2 * SLOTS, WIDTH), BF16), vmem((2 * SLOTS, WIDTH), BF16),
            vmem((2, TOK, WIDTH), F32),
            vmem((ND, 2 * ROWS_DP, WIDTH), F32), vmem((ND, 2 * ROWS_DP, WIDTH), F32),
            vmem((ROWS_DP, WIDTH), BF16), vmem((ROWS_DP, WIDTH), BF16),
            vmem((WIDTH, HID), BF16), vmem((WIDTH, HID), BF16),
            dma((10,)), dma((4,)),
            dma((STREAMS, len(SUMS), LINKS)), dma((STREAMS, len(SUMS), LINKS)),
            dma((STREAMS, len(GATHERS), LINKS)), dma((STREAMS, len(GATHERS), LINKS)),
            dma((NE,)), dma((NE,)), dma((NE,)), dma((NE,)), dma((ND,)), dma((ND,)),
        ],
        compiler_params=pltpu.CompilerParams(
            collective_id=0, has_side_effects=True, vmem_limit_bytes=60 * 1024 * 1024
        ),
    )(*args)
    return pl.pallas_call(
        place,
        out_shape=tuple(jax.ShapeDtypeStruct(part.shape, part.dtype) for part in results),
        in_specs=[any_spec] * 4,
        out_specs=(hbm_spec,) * 4,
        scratch_shapes=[vmem(part.shape, part.dtype) for part in results] + [dma((2, 4))],
        compiler_params=pltpu.CompilerParams(vmem_limit_bytes=60 * 1024 * 1024),
    )(*results)


def solution(mesh):
    placed = (
        P("expert", "ffn"),
        P("expert", "ffn"),
        P("expert", None),
        P("expert"),
        P("expert", "ffn", "dp"),
        P("expert", "ffn", "dp"),
        P("expert", "dp", "ffn"),
        P("ffn", "dp"),
        P("ffn", "dp"),
        P("dp", "ffn"),
    )
    return jax.shard_map(
        per_device,
        mesh=mesh,
        in_specs=placed,
        out_specs=(
            P(("expert", "dp"), "ffn"),
            P(("expert", "dp"), "ffn"),
            P("expert", "ffn", "dp"),
            P("expert", "ffn", "dp"),
        ),
        check_vma=False,
    )
```

```python
import functools
from typing import NamedTuple

import jax
import jax.numpy as jnp
from jax import lax
from jax.experimental import pallas as pl
from jax.experimental.pallas import tpu as pltpu
from jax.sharding import PartitionSpec as P

MESH = pl.DeviceIdType.MESH
F32 = jnp.float32
BF16 = jnp.bfloat16

TOK = 96
CAP = 24
NE = 8
NF = 16
ND = 8
SLOTS = NE * CAP
WIDTH = 320
HID = 1024
SUB = 48
COL = 128
STREAMS = 3
SOURCES = ((0, 2, 4, 6), (1, 3, 5, 7))
LINKS = 8
CHAINS = 4


class Ring(NamedTuple):
    sums: tuple
    sum_at: tuple
    sum_time: float
    gathers: tuple
    gather_at: tuple
    gather_time: float
    lead: float
    late: float


RINGS = (
    Ring(
        ((0, 8, 4), (1, 7, 3), (0, 3, 1), (1, 2, 1)), (0.0, 0.01, 0.2, 1.2), 6.5,
        ((0, 4, 8), (1, 4, 7), (0, 1, 3), (1, 1, 3)), (0.0, 0.01, 0.02, 0.03), 5.5,
        3, 1,
    ),
    Ring(
        ((0, 8, 4), (1, 7, 3), (0, 3, 1), (1, 2, 1)), (0.0, 0.01, 0.2, 1.2), 6.5,
        ((0, 1, 8), (1, 1, 7)), (0.0, 0.01), 8,
        3, 2,
    ),
)
JUMPS = sorted({1} | {near for ring in RINGS for _, _, near in ring.sums} | {near for ring in RINGS for _, near, _ in ring.gathers})
ROWS_DP = TOK // ND
PARTNERS = ((0, 0, 1),) + tuple((dy, flip, swap) for dy, flip in ((1, 0), (1, 1), (-1, 0), (2, 1)) for swap in (0, 1))


def dot(a, b):
    return lax.dot_general(a, b, (((1,), (0,)), ((), ())), preferred_element_type=F32)


def dot_last(a, b):
    return lax.dot_general(a, b, (((1,), (1,)), ((), ())), preferred_element_type=F32)


def dot_first(a, b):
    return lax.dot_general(a, b, (((0,), (0,)), ((), ())), preferred_element_type=F32)


def kernel(
    tok_hbm, cot_hbm, routing_hbm, gate_hbm, eg_hbm, eu_hbm, ed_hbm, sg_hbm, su_hbm, sd_hbm,
    lo_hbm, gt_hbm, gg_hbm, gu_hbm,
    tok, cot, routing, gate, eg, eu, ed, sg, su, sd,
    outbox, inbox, routed_in, routed_cot, part_s, part_r,
    stage, held, act_s, act_r,
    outbox2, inbox2, term, outbox3, inbox3, lo, gt, gg, gu,
    load_sem, store_sem, rs_send, rs_recv, ag_send, ag_recv, x_send, x_recv, y_send, y_recv, z_send, z_recv,
):
    me_e, me_f, me_d = lax.axis_index("expert"), lax.axis_index("ffn"), lax.axis_index("dp")
    y_hi, core = lax.div(me_e, 2), lax.rem(me_e, 2)
    y_lo = lax.rem(me_d, 2)
    other_d = me_d + 1 - 2 * y_lo
    toward = 2 * y_lo - 1

    def way_of(way, stream):
        return 1 - way if stream == STREAMS - 1 else way

    def along(way, distance):
        return lax.rem(me_f + (distance if way == 0 else NF - distance), NF)

    def expert_at(dy, swap):
        return 2 * lax.rem(y_hi + dy + 4, 4) + (core if swap == 0 else 1 - core)

    barrier = pltpu.get_barrier_semaphore()
    for jump in JUMPS:
        for way in range(2):
            pl.semaphore_signal(
                barrier, inc=1, device_id={"ffn": along(way, jump)}, device_id_type=MESH
            )
    for dy, flip, swap in PARTNERS:
        pl.semaphore_signal(
            barrier, inc=1,
            device_id={"expert": expert_at(dy * toward, swap), "dp": other_d if flip else me_d}, device_id_type=MESH,
        )
    for k in range(1, ND):
        pl.semaphore_signal(
            barrier, inc=1, device_id={"dp": lax.rem(me_d + k, ND)}, device_id_type=MESH
        )

    loads = [
        pltpu.make_async_copy(src, dst, load_sem.at[n])
        for n, (src, dst) in enumerate(
            [
                (routing_hbm, routing), (gate_hbm, gate), (tok_hbm, tok), (cot_hbm, cot),
                (sg_hbm, sg), (su_hbm, su), (sd_hbm, sd),
                (eg_hbm.at[0], eg), (eu_hbm.at[0], eu), (ed_hbm.at[0], ed),
            ]
        )
    ]
    for load in loads:
        load.start()

    for n in range(4):
        loads[n].wait()

    same = (
        lax.broadcasted_iota(jnp.int32, (TOK, TOK), 0) == lax.broadcasted_iota(jnp.int32, (TOK, TOK), 1)
    )

    def column(row):
        across = jnp.broadcast_to(row.astype(F32).reshape(1, TOK), (TOK, TOK))
        return jnp.sum(jnp.where(same, across, 0.0), axis=1, keepdims=True)

    gate_column = column(gate[...])
    chosen = routing[...].reshape(1, TOK)
    onehot = (chosen == lax.broadcasted_iota(jnp.int32, (NE, TOK), 0)).astype(F32)
    before = (
        lax.broadcasted_iota(jnp.int32, (TOK, TOK), 0) < lax.broadcasted_iota(jnp.int32, (TOK, TOK), 1)
    )
    earlier = dot(onehot.astype(BF16), before.astype(BF16))
    slot = jnp.sum(earlier * onehot, axis=0, keepdims=True)
    target = chosen * (2 * CAP) + slot.astype(jnp.int32)
    boxes = lax.broadcasted_iota(jnp.int32, (2 * SLOTS, TOK), 0)
    pick_first = (boxes == target).astype(BF16)
    pick_second = (boxes == target + CAP).astype(BF16)
    scaled = (gate_column * cot[...].astype(F32)).astype(BF16)
    outbox[...] = (dot(pick_first, tok[...]) + dot(pick_second, scaled)).astype(BF16)

    pl.semaphore_wait(barrier, 2 * len(JUMPS) + len(PARTNERS) + (ND - 1))

    def box(ref, index):
        return ref.at[pl.ds(pl.multiple_of(index * 2 * CAP, 2 * CAP), 2 * CAP)]

    routes = [(0, 0, 1)] + [
        (dy, flip, swap) for dy, flip in ((toward, 1), (toward, 0), (2, 1)) for swap in range(2)
    ]

    def tokens_out(n):
        dy, flip, swap = routes[n]
        peer = expert_at(dy, swap)
        return pltpu.make_async_remote_copy(
            src_ref=box(outbox, peer), dst_ref=box(inbox, me_e),
            send_sem=x_send.at[n], recv_sem=x_recv.at[n],
            device_id={"expert": peer, "dp": other_d if flip else me_d}, device_id_type=MESH,
        )

    def tokens_in(n):
        dy, flip, swap = routes[n]
        peer = expert_at(dy if flip else -dy, swap)
        return pltpu.make_async_remote_copy(
            src_ref=box(outbox, me_e), dst_ref=box(inbox, peer),
            send_sem=x_send.at[n], recv_sem=x_recv.at[n],
            device_id={"expert": peer, "dp": other_d if flip else me_d}, device_id_type=MESH,
        )

    for n in range(len(routes)):
        tokens_out(n).start()
    box(inbox, me_e)[...] = box(outbox, me_e)[...]

    for n in range(4, 7):
        loads[n].wait()
    part_s[0] = dot(tok[...], sg[...])
    part_s[1] = dot(tok[...], su[...])
    part_s[2] = dot(cot[...], sd[...])

    def block(ref, stream, owner):
        columns = pl.ds(pl.multiple_of(lax.div(owner, 2) * COL, COL), COL)
        half = lax.rem(owner, 2)
        first = half * SUB + (0 if stream == 0 else (stream - 1) * 2 * SUB)
        return ref.at[:, pl.ds(pl.multiple_of(first, SUB), SUB), columns]

    def mine(stream):
        return (part_s if stream == 0 else part_r), (act_s if stream == 0 else act_r)

    def sum_copy(ring, stream, chain, step):
        way, far, near = ring.sums[chain]
        way = way_of(way, stream)
        return pltpu.make_async_remote_copy(
            src_ref=stage.at[stream, chain, step], dst_ref=held.at[stream, chain, step],
            send_sem=rs_send.at[stream, chain, step], recv_sem=rs_recv.at[stream, chain, step],
            device_id={"ffn": along(way, 1 if step < far - near else near)}, device_id_type=MESH,
        )

    def sum_step(ring, stream, chain, step):
        way, far, _ = ring.sums[chain]
        way = way_of(way, stream)
        value = block(mine(stream)[0], stream, along(way, far - step))[...]
        if step > 0:
            sum_copy(ring, stream, chain, step - 1).wait_recv()
            value = value + held[stream, chain, step - 1].astype(F32)
        stage[stream, chain, step] = value.astype(BF16)
        sum_copy(ring, stream, chain, step).start()

    def sum_end(ring, stream):
        part, act = mine(stream)
        value = block(part, stream, me_f)[...]
        for chain, (_, far, near) in sorted(enumerate(ring.sums), reverse=True):
            sum_copy(ring, stream, chain, far - near).wait_recv()
            value = value + held[stream, chain, far - near].astype(F32)
        g, u, p = value[0], value[1], value[2]
        squash = jax.nn.sigmoid(g)
        silu = g * squash
        own = block(act, stream, me_f)
        own[0] = (silu * u).astype(BF16)
        own[1] = (p * u * squash * (1.0 + g * (1.0 - squash))).astype(BF16)
        own[2] = (p * silu).astype(BF16)

    def gather_copy(ring, stream, chain, step, distance):
        way, near, _ = ring.gathers[chain]
        way = way_of(way, stream)
        ref = block(mine(stream)[1], stream, along(1 - way, distance))
        return pltpu.make_async_remote_copy(
            src_ref=ref, dst_ref=ref,
            send_sem=ag_send.at[stream, chain, step], recv_sem=ag_recv.at[stream, chain, step],
            device_id={"ffn": along(way, near if step == 0 else 1)}, device_id_type=MESH,
        )

    def gather_out(ring, stream, chain, step):
        return gather_copy(ring, stream, chain, step, 0 if step == 0 else ring.gathers[chain][1] + step - 1)

    def gather_arrived(ring, stream, chain, step):
        gather_copy(ring, stream, chain, step, ring.gathers[chain][1] + step).wait_recv()

    def gather_step(ring, stream, chain, step):
        if step > 0:
            gather_arrived(ring, stream, chain, step - 1)
        gather_out(ring, stream, chain, step).start()

    def gather_end(ring, stream):
        for chain, (_, near, far) in sorted(enumerate(ring.gathers), reverse=True):
            gather_arrived(ring, stream, chain, far - near)

    def routed_terms():
        for n in range(len(routes)):
            tokens_in(n).wait_recv()
        came = inbox[...].astype(F32)
        routed_in[...] = jnp.concatenate(
            [came[2 * CAP * e : 2 * CAP * e + CAP] for e in SOURCES[0] + SOURCES[1]], axis=0
        ).astype(BF16)
        routed_cot[...] = jnp.concatenate(
            [came[2 * CAP * e + CAP : 2 * CAP * (e + 1)] for e in SOURCES[0] + SOURCES[1]], axis=0
        ).astype(BF16)
        for n in range(7, 10):
            loads[n].wait()
        part_r[0] = dot(routed_in[...], eg[...])
        part_r[1] = dot(routed_in[...], eu[...])
        part_r[2] = dot(routed_cot[...], ed[...])

    def result_copy(part, dy):
        peer = 2 * lax.rem(y_hi + dy, 4) + part
        swap = lax.rem(core + part, 2)
        place = (1, 2 + 2 * y_lo + swap, 6 + swap, 2 + 2 * y_lo + swap)[dy]
        where = (me_d, me_d - y_lo, other_d, me_d - y_lo + 1)[dy]
        return pltpu.make_async_remote_copy(
            src_ref=box(outbox2, peer), dst_ref=box(inbox2, place),
            send_sem=y_send.at[2 * dy + part], recv_sem=y_recv.at[place],
            device_id={"expert": peer, "dp": where}, device_id_type=MESH,
        )

    def result_arrived(n):
        pltpu.make_async_remote_copy(
            src_ref=box(outbox2, n), dst_ref=box(inbox2, n),
            send_sem=y_send.at[n], recv_sem=y_recv.at[n],
            device_id={"expert": expert_at(0, 1)}, device_id_type=MESH,
        ).wait_recv()

    def routed_results(part):
        rows = slice(part * 2 * SUB, (part + 1) * 2 * SUB)
        routed_out = dot_last(act_r[0, rows], ed[...])
        routed_back = dot_last(act_r[1, rows], eg[...]) + dot_last(act_r[2, rows], eu[...])
        for n, e in enumerate(SOURCES[part]):
            outbox2[2 * CAP * e : 2 * CAP * (e + 1)] = jnp.concatenate(
                [routed_out[CAP * n : CAP * (n + 1)], routed_back[CAP * n : CAP * (n + 1)]], axis=0
            ).astype(BF16)

        for dy in range(1, 4):
            result_copy(part, dy).start()

        @pl.when(core != part)
        def _():
            result_copy(part, 0).start()

        @pl.when(core == part)
        def _():
            inbox2[: 2 * CAP] = box(outbox2, me_e)[...]

    def run(ring):
        begins = (0, ring.lead + 0.1, ring.lead + 0.2)
        routed_end = ring.lead + ring.sum_time + ring.gather_time + 0.2
        plan = [(ring.lead - 0.5, "Rterms", routed_terms)]
        for stream, begin in enumerate(begins):
            second = begin + ring.sum_time if stream > 0 else routed_end - ring.gather_time + ring.late
            if stream > 0:
                results = functools.partial(routed_results, stream - 1)
                plan.append((second + ring.gather_time + 0.05, f"Rout{stream}", results))
            plan.append((begin + ring.sum_time - 0.05, f"Aend{stream}", functools.partial(sum_end, ring, stream)))
            plan.append((second + ring.gather_time, f"Gend{stream}", functools.partial(gather_end, ring, stream)))
            for chain, (_, far, near) in enumerate(ring.sums):
                for step in range(far - near + 1):
                    when = begin + ring.sum_at[chain] + step
                    plan.append((when, f"A{stream}{chain}{step}", functools.partial(sum_step, ring, stream, chain, step)))
            for chain, (_, near, far) in enumerate(ring.gathers):
                for step in range(far - near + 1):
                    when = second + ring.gather_at[chain] + step
                    plan.append((when, f"G{stream}{chain}{step}", functools.partial(gather_step, ring, stream, chain, step)))
        for _, name, act in sorted(plan, key=lambda entry: entry[0]):
            act()

    for side in range(2):
        pl.when(core == side)(functools.partial(run, RINGS[side]))

    shared_out = dot_last(act_s[0], sd[...])
    shared_back = dot_last(act_s[1], sg[...]) + dot_last(act_s[2], su[...])
    senders = [me_e, expert_at(0, 1)] + [expert_at(toward, n % 2) for n in range(4)] + [expert_at(2, n) for n in range(2)]
    columns = lax.broadcasted_iota(jnp.int32, (1, 2 * SLOTS), 1)
    sender = jnp.zeros((1, 2 * SLOTS), jnp.int32)
    for n in range(NE):
        here = (columns >= 2 * CAP * n) & (columns < 2 * CAP * (n + 1))
        sender = jnp.where(here, senders[n], sender)
    row = lax.rem(columns, 2 * CAP)
    slot_column = column(slot).astype(jnp.int32)
    of_sender = column(chosen).astype(jnp.int32) == sender
    take_first = (of_sender & (row == slot_column)).astype(BF16)
    take_second = (of_sender & (row == slot_column + CAP)).astype(BF16)
    for n in range(1, NE):
        result_arrived(n)
    term[0] = gate_column * dot(take_first, inbox2[...]) + shared_out
    term[1] = dot(take_second, inbox2[...]) + shared_back
    for d in range(ND):
        outbox3[d, :ROWS_DP] = term[0, ROWS_DP * d : ROWS_DP * (d + 1)]
        outbox3[d, ROWS_DP:] = term[1, ROWS_DP * d : ROWS_DP * (d + 1)]

    def dp_send(k):
        peer = lax.rem(me_d + k, ND)
        return pltpu.make_async_remote_copy(
            src_ref=outbox3.at[peer], dst_ref=inbox3.at[k],
            send_sem=z_send.at[k], recv_sem=z_recv.at[k],
            device_id={"dp": peer}, device_id_type=MESH,
        )

    for k in range(1, ND):
        dp_send(k).start()

    gg[...] = dot_first(routed_in[...], act_r[1]).astype(BF16)
    gu[...] = dot_first(routed_in[...], act_r[2]).astype(BF16)
    stores = [
        pltpu.make_async_copy(gg, gg_hbm.at[0], store_sem.at[0]),
        pltpu.make_async_copy(gu, gu_hbm.at[0], store_sem.at[1]),
    ]
    for store in stores:
        store.start()

    total = outbox3[me_d]
    for k in range(1, ND):
        dp_send(k).wait_recv()
        total = total + inbox3[k]
    lo[...] = total[:ROWS_DP].astype(BF16)
    gt[...] = total[ROWS_DP:].astype(BF16)
    last = [
        pltpu.make_async_copy(lo, lo_hbm, store_sem.at[2]),
        pltpu.make_async_copy(gt, gt_hbm, store_sem.at[3]),
    ]
    for store in last:
        store.start()
    def all_sent(ring):
        for stream in range(STREAMS):
            for chain, (_, far, near) in enumerate(ring.sums):
                for step in range(far - near + 1):
                    sum_copy(ring, stream, chain, step).wait_send()
            for chain, (_, near, far) in enumerate(ring.gathers):
                for step in range(far - near + 1):
                    gather_out(ring, stream, chain, step).wait_send()

    for side in range(2):
        pl.when(core == side)(functools.partial(all_sent, RINGS[side]))
    for n in range(len(routes)):
        tokens_out(n).wait_send()
    for part in range(2):
        for dy in range(1, 4):
            result_copy(part, dy).wait_send()

        @pl.when(core != part)
        def _(part=part):
            result_copy(part, 0).wait_send()

    for k in range(1, ND):
        dp_send(k).wait_send()
    for store in stores + last:
        store.wait()


def place(*refs):
    n = (len(refs) - 1) // 3
    sources, results, held, sem = refs[:n], refs[n : 2 * n], refs[2 * n : 3 * n], refs[-1]
    reads = [pltpu.make_async_copy(sources[k], held[k], sem.at[0, k]) for k in range(n)]
    writes = [pltpu.make_async_copy(held[k], results[k], sem.at[1, k]) for k in range(n)]
    for read in reads:
        read.start()
    for read, write in zip(reads, writes):
        read.wait()
        write.start()
    for write in writes:
        write.wait()


def per_device(tokens, cotangent, routing, gate_value, eg, eu, ed, sg, su, sd):
    args = (
        tokens, cotangent, routing.reshape(TOK), gate_value,
        eg, eu, jnp.swapaxes(ed, 1, 2), sg, su, jnp.swapaxes(sd, 0, 1),
    )
    vmem = pltpu.VMEM
    dma = pltpu.SemaphoreType.DMA
    any_spec = pl.BlockSpec(memory_space=pl.ANY)
    hbm_spec = pl.BlockSpec(memory_space=pltpu.HBM)
    results = pl.pallas_call(
        kernel,
        out_shape=(
            jax.ShapeDtypeStruct((ROWS_DP, WIDTH), BF16),
            jax.ShapeDtypeStruct((ROWS_DP, WIDTH), BF16),
            jax.ShapeDtypeStruct((1, WIDTH, HID), BF16),
            jax.ShapeDtypeStruct((1, WIDTH, HID), BF16),
        ),
        in_specs=[hbm_spec] * 10,
        out_specs=(any_spec,) * 4,
        scratch_shapes=[
            vmem((TOK, WIDTH), BF16), vmem((TOK, WIDTH), BF16), vmem((TOK,), jnp.int32), vmem((TOK,), F32),
            vmem((WIDTH, HID), BF16), vmem((WIDTH, HID), BF16), vmem((WIDTH, HID), BF16),
            vmem((WIDTH, HID), BF16), vmem((WIDTH, HID), BF16), vmem((WIDTH, HID), BF16),
            vmem((2 * SLOTS, WIDTH), BF16), vmem((2 * SLOTS, WIDTH), BF16),
            vmem((SLOTS, WIDTH), BF16), vmem((SLOTS, WIDTH), BF16),
            vmem((3, TOK, HID), F32), vmem((3, SLOTS, HID), F32),
            vmem((STREAMS, CHAINS, LINKS, 3, SUB, COL), BF16),
            vmem((STREAMS, CHAINS, LINKS, 3, SUB, COL), BF16),
            vmem((3, TOK, HID), BF16), vmem((3, SLOTS, HID), BF16),
            vmem((2 * SLOTS, WIDTH), BF16), vmem((2 * SLOTS, WIDTH), BF16),
            vmem((2, TOK, WIDTH), F32),
            vmem((ND, 2 * ROWS_DP, WIDTH), F32), vmem((ND, 2 * ROWS_DP, WIDTH), F32),
            vmem((ROWS_DP, WIDTH), BF16), vmem((ROWS_DP, WIDTH), BF16),
            vmem((WIDTH, HID), BF16), vmem((WIDTH, HID), BF16),
            dma((10,)), dma((4,)),
            dma((STREAMS, CHAINS, LINKS)), dma((STREAMS, CHAINS, LINKS)),
            dma((STREAMS, CHAINS, LINKS)), dma((STREAMS, CHAINS, LINKS)),
            dma((NE,)), dma((NE,)), dma((NE,)), dma((NE,)), dma((ND,)), dma((ND,)),
        ],
        compiler_params=pltpu.CompilerParams(
            collective_id=0, has_side_effects=True, vmem_limit_bytes=60 * 1024 * 1024
        ),
    )(*args)
    return pl.pallas_call(
        place,
        out_shape=tuple(jax.ShapeDtypeStruct(part.shape, part.dtype) for part in results),
        in_specs=[any_spec] * 4,
        out_specs=(hbm_spec,) * 4,
        scratch_shapes=[vmem(part.shape, part.dtype) for part in results] + [dma((2, 4))],
        compiler_params=pltpu.CompilerParams(vmem_limit_bytes=60 * 1024 * 1024),
    )(*results)


def solution(mesh):
    placed = (
        P("expert", "ffn"),
        P("expert", "ffn"),
        P("expert", None),
        P("expert"),
        P("expert", "ffn", "dp"),
        P("expert", "ffn", "dp"),
        P("expert", "dp", "ffn"),
        P("ffn", "dp"),
        P("ffn", "dp"),
        P("dp", "ffn"),
    )
    return jax.shard_map(
        per_device,
        mesh=mesh,
        in_specs=placed,
        out_specs=(
            P(("expert", "dp"), "ffn"),
            P(("expert", "dp"), "ffn"),
            P("expert", "ffn", "dp"),
            P("expert", "ffn", "dp"),
        ),
        check_vma=False,
    )
```
